128 devices in a mesh: lat: 8 (over x, y_lo), lon: 16 (over z, y_hi, core).
Axes of the slice: x: 4, y: 4 (y_hi: 2, y_lo: 2; y = y_hi * 2 + y_lo), z: 4, core: 2. Of those that a mesh axis runs over, the one named last changes fastest.
Arguments:
- latents: float32 [4, 144, 192, 512], P(None, 'lat', 'lon'), may hold values from -80 to 80
- qkv_weight: bfloat16 [512, 1536], replicated, may hold values from -0.35 to 0.35
- proj_weight: bfloat16 [512, 512], replicated, may hold values from -0.25 to 0.25
- up_weight: bfloat16 [512, 2048], replicated, may hold values from -0.25 to 0.25
- down_weight: bfloat16 [2048, 512], replicated, may hold values from -0.125 to 0.125
- modulation: float32 [2, 2, 512], replicated, may hold values from -2.5 to 2.5
Outputs:
- updated: float32 [4, 144, 192, 512], P(None, 'lat', 'lon')
The draws below stay inside these ranges and needn't reach their ends.
All inputs are finite; a program needn't handle non-finite values.
Results may differ from the reference program's by a relative error of at most 0.0045.
Values may be sent and summed in bfloat16 or wider, within the bound.
A program may use at most 128 MiB of HBM per device.

```python
import jax
import jax.numpy as jnp
from jax import lax

D = 512
HEADS = 16
FFH = 2048
LEVELS = 4
WLEV = 2
WLAT = 6
WLON = 12
NLAT = 144
NLON = 192


def draw_latents(key, part):
    key = jax.random.fold_in(key, 11)
    key_z, key_r, key_c = jax.random.split(key, 3)
    shape = (LEVELS, NLAT, NLON, D)
    row_scale = jnp.exp(jax.random.uniform(key_r, (LEVELS, NLAT, NLON, 1), jnp.float32, -1.2, 1.1))
    col_scale = jnp.exp(jax.random.uniform(key_c, (D,), jnp.float32, -1.2, 1.1))
    base = jnp.clip(jax.random.normal(key_z, shape, jnp.float32), -4.0, 4.0)
    values = base * row_scale * col_scale
    return jnp.clip(values, -80.0, 80.0)


def draw_qkv_weight(key, part):
    key = jax.random.fold_in(key, 23)
    spread = D ** (-0.5)
    values = jnp.clip(jax.random.normal(key, (D, 3 * D), jnp.float32), -6.0, 6.0) * spread
    return jnp.clip(values, -0.35, 0.35).astype(jnp.bfloat16)


def normal_values(rng, dims, scale, reach, kind=jnp.bfloat16):
    result = scale * jax.random.normal(rng, dims, jnp.float32)
    return jnp.clip(result, min=-reach, max=reach).astype(kind)


def setup_inputs(seed: int = 0) -> dict:
    arg_keys = jax.random.split(jax.random.key(seed), 7)
    return {
        "latents": draw_latents(jax.random.fold_in(arg_keys[6], 71), 0),
        "qkv_weight": draw_qkv_weight(jax.random.fold_in(arg_keys[6], 71), 0),
        "proj_weight": normal_values(arg_keys[2], (D, D), D ** -0.5, 0.25),
        "up_weight": normal_values(arg_keys[3], (D, FFH), D ** -0.5, 0.25),
        "down_weight": normal_values(arg_keys[4], (FFH, D), FFH ** -0.5, 0.125),
        "modulation": normal_values(arg_keys[5], (2, 2, D), 0.5, 2.5, jnp.float32),
    }


def norm_mod(values, params):
    feat_mean = lax.optimization_barrier(jnp.mean(values, axis=-1, keepdims=True))
    centered = values - feat_mean
    feat_var = lax.optimization_barrier(jnp.mean(centered * centered, axis=-1, keepdims=True))
    scaled = centered * lax.rsqrt(feat_var + 1e-05)
    return (scaled * (1.0 + params[0]) + params[1]).astype(jnp.bfloat16)

def to_windows(array):
    levels_n, rows_n, cols_n = array.shape[:3]
    trailing = array.shape[3:]
    shaped = array.reshape((levels_n // WLEV, WLEV, rows_n // WLAT, WLAT, cols_n // WLON, WLON) + trailing)
    axes_order = (0, 2, 4, 1, 3, 5) + tuple(range(6, 6 + len(trailing)))
    return shaped.transpose(axes_order).reshape((-1, WLEV * WLAT * WLON) + trailing)

def from_windows(array, levels_n, rows_n, cols_n):
    trailing = array.shape[2:]
    shaped = array.reshape((levels_n // WLEV, rows_n // WLAT, cols_n // WLON, WLEV, WLAT, WLON) + trailing)
    axes_order = (0, 3, 1, 4, 2, 5) + tuple(range(6, 6 + len(trailing)))
    return shaped.transpose(axes_order).reshape((levels_n, rows_n, cols_n) + trailing)

def attend(window_in, labels, qkv_weight, proj_weight):
    levels_n, rows_n, cols_n, width = window_in.shape
    tokens = to_windows(window_in)
    label_win = to_windows(labels[..., None])[..., 0]
    count_win, span = (tokens.shape[0], tokens.shape[1])
    qkv_rows = jnp.dot(tokens.reshape(-1, width), qkv_weight, preferred_element_type=jnp.float32).astype(jnp.bfloat16)
    qkv_rows = qkv_rows.reshape(count_win, span, 3, HEADS, width // HEADS).astype(jnp.float32)
    scores = jnp.einsum('nqhe,nkhe->nhqk', qkv_rows[:, :, 0], qkv_rows[:, :, 1]) * (width // HEADS) ** (-0.5)
    allowed = label_win[:, None, :, None] == label_win[:, None, None, :]
    scores = jnp.where(allowed, scores, jnp.float32(-1e+30))
    attn_prob = jax.nn.softmax(scores, axis=-1).astype(jnp.bfloat16)
    context = jnp.einsum('nhqk,nkhe->nqhe', attn_prob.astype(jnp.float32), qkv_rows[:, :, 2]).astype(jnp.bfloat16)
    projected = jnp.dot(context.reshape(-1, width), proj_weight, preferred_element_type=jnp.float32)
    return from_windows(projected.reshape(count_win, span, width), levels_n, rows_n, cols_n)

def reference(latents, qkv_weight, proj_weight, up_weight, down_weight, modulation):
    levels_n, nlat_all, nlon_all, width = latents.shape
    rolled = jnp.roll(latents, (-1, -(WLAT // 2), -(WLON // 2)), axis=(0, 1, 2))
    bands = rolled.reshape(levels_n, nlat_all // WLAT, WLAT, nlon_all, width).transpose(1, 0, 2, 3, 4)
    level_flag = (jnp.arange(levels_n) >= levels_n - 1).astype(jnp.int32)

    def one_band(operands):
        band, band_idx = operands
        row_index = band_idx * WLAT + jnp.arange(WLAT, dtype=jnp.int32)
        lat_flag = (row_index >= nlat_all - WLAT // 2).astype(jnp.int32)
        labels = 2 * lat_flag[None, :, None] + level_flag[:, None, None]
        labels = jnp.broadcast_to(labels, (levels_n, WLAT, nlon_all)).astype(jnp.int32)
        normed = norm_mod(band, modulation[0])
        mid = band + attend(normed, labels, qkv_weight, proj_weight)
        normed_two = norm_mod(mid, modulation[1])
        up_part = jnp.dot(normed_two.reshape(-1, width), up_weight, preferred_element_type=jnp.float32)
        hidden = jax.nn.gelu(up_part, approximate=False).astype(jnp.bfloat16)
        down_part = jnp.dot(hidden, down_weight, preferred_element_type=jnp.float32)
        return mid + down_part.reshape(mid.shape)
    results = lax.map(one_band, (bands, jnp.arange(nlat_all // WLAT, dtype=jnp.int32)))
    results = results.transpose(1, 0, 2, 3, 4).reshape(levels_n, nlat_all, nlon_all, width)
    return jnp.roll(results, (1, WLAT // 2, WLON // 2), axis=(0, 1, 2))
```

```python
import functools
import math

import jax
import jax.numpy as jnp
import numpy as np
from jax import lax
from jax.experimental import pallas as pl
from jax.experimental.pallas import tpu as pltpu
from jax.sharding import PartitionSpec as P

HEADS = 16
D = 512
FFH = 2048
HID = 512
NEG = -1e30
BF = jnp.bfloat16
F32 = jnp.float32
MESH = pl.DeviceIdType.MESH
LEV = ((1, 2), (3, 0))
ROWS_A, ROWS_B, ROWS_C, ROWS_T = range(3, 9), range(9, 15), range(15, 18), range(0, 3)


def unit_tokens():
    return (
        [(0, c) for c in range(8)]
        + [(1, c) for c in range(8)]
        + [(0, c) for c in range(8, 12)]
        + [(1, c) for c in range(8, 12)]
    )


def half_order(rows, left):
    cols = range(0, 6) if left else range(6, 12)
    return [(s, r, c) for s in range(2) for r in range(rows) for c in cols]


@functools.cache
def tables():
    unit = unit_tokens()

    def src(rows):
        return {(s, r, c): r * 24 + i for r in range(rows) for i, (s, c) in enumerate(unit)}

    six, three = src(6), src(3)
    pa = np.zeros((144, 144), np.float32)
    for h in range(2):
        for i, t in enumerate(half_order(6, h == 0)):
            pa[h * 72 + i, six[t]] = 1
    pc = np.zeros((160, 144), np.float32)
    for h in range(2):
        for g in range(2):
            for i, t in enumerate(half_order(3, h == 0)):
                pc[h * 80 + g * 40 + i, g * 72 + three[t]] = 1
    ia = np.zeros((288, 288), np.float32)
    for h in range(2):
        for g in range(2):
            for i, t in enumerate(half_order(6, h == 1)):
                ia[g * 144 + six[t], h * 144 + g * 72 + i] = 1
    ic = np.zeros((288, 320), np.float32)
    for part in range(2):
        for h in range(2):
            for g in range(2):
                for i, t in enumerate(half_order(3, h == 1)):
                    ic[part * 144 + g * 72 + three[t], part * 160 + h * 80 + g * 40 + i] = 1
    lev = np.tile(np.repeat(np.arange(2), 36), 2)
    bias = np.where(lev[:, None] == lev[None, :], 0.0, NEG)
    off = np.tile(np.arange(40), 4)
    pad, lev, part = off >= 36, off // 18, np.repeat(np.arange(2), 80)
    bias_s = np.zeros((4, 160, 160))
    for g in range(2):
        for last in range(2):
            ok = np.broadcast_to(~pad[None, :], (160, 160)).copy()
            if g:
                ok &= (lev[:, None] == lev[None, :]) | pad[:, None]
            if last:
                ok &= part[:, None] == part[None, :]
            bias_s[last * 2 + g] = np.where(ok, 0.0, NEG)
    return (
        pa.astype(jnp.bfloat16), pc.astype(jnp.bfloat16), ia.astype(jnp.bfloat16),
        ic.astype(jnp.bfloat16), bias.astype(np.float32), bias_s.astype(np.float32),
    )


def dot(a, b):
    return jnp.dot(a, b, preferred_element_type=F32)


def norm_mod(v, mod):
    mean = jnp.sum(v, axis=-1, keepdims=True) * (1.0 / D)
    c = v - mean
    var = jnp.sum(c * c, axis=-1, keepdims=True) * (1.0 / D)
    return (c * lax.rsqrt(var + 1e-5)) * (1.0 + mod[0:1]) + mod[1:2]


def gelu(u):
    return 0.5 * u * (1.0 + lax.erf(u * (1.0 / math.sqrt(2.0))))


def kernel(
    nlat, nlon,
    lat_hbm, wqkv_hbm, wproj_hbm, wup_hbm, wdown_hbm, mod_hbm,
    pa_hbm, pc_hbm, ia_hbm, ic_hbm, bias_hbm, bias_s_hbm,
    out_hbm,
    x, wqkv, wproj, wup, wdown, mod, pa, pc, ia, ic, bias, bias_s,
    nbuf, send_a, send_s, own_a, own_c, recv_a, recv_s,
    qkv, ctx, keep_a, keep_c, back_a, back_s, home_a, home_s, n2,
    in_sem, w_sem, out_sem, ss, rs,
):
    d, j = lax.axis_index("lat"), lax.axis_index("lon")
    up_d, dn_d = lax.rem(d + 1, nlat), lax.rem(d + nlat - 1, nlat)
    rt, lf = lax.rem(j + 1, nlon), lax.rem(j + nlon - 1, nlon)
    barrier = pltpu.get_barrier_semaphore()
    for who in ((d, rt), (d, lf), (up_d, j), (dn_d, j), (up_d, rt), (dn_d, lf)):
        pl.semaphore_signal(barrier, inc=1, device_id=who, device_id_type=MESH)

    loads = []
    mod_cp = pltpu.make_async_copy(mod_hbm, mod, w_sem.at[0])
    mod_cp.start()
    classes = ((3, 6), (9, 6), (15, 3), (0, 3))
    for k, (r0, n) in enumerate(classes):
        cps = []
        for g in range(2):
            for s in range(2):
                lev = LEV[g][s]
                cps.append(pltpu.make_async_copy(
                    lat_hbm.at[lev, pl.ds(r0, n), pl.ds(0, 8)],
                    x.at[g, pl.ds(r0, n), pl.ds(8 * s, 8)], in_sem.at[k, g, s, 0]))
                cps.append(pltpu.make_async_copy(
                    lat_hbm.at[lev, pl.ds(r0, n), pl.ds(8, 4)],
                    x.at[g, pl.ds(r0, n), pl.ds(16 + 4 * s, 4)], in_sem.at[k, g, s, 1]))
        for c in cps:
            c.start()
        loads.append(cps)
    wcp = {}
    for i, (a, b) in enumerate((
        (pa_hbm, pa), (pc_hbm, pc), (wqkv_hbm, wqkv), (bias_hbm, bias), (bias_s_hbm, bias_s),
        (ia_hbm, ia), (ic_hbm, ic), (wproj_hbm, wproj), (wup_hbm, wup), (wdown_hbm, wdown),
    )):
        c = pltpu.make_async_copy(a, b, w_sem.at[i + 1])
        c.start()
        wcp[i] = c

    def remote(src, dst, n, who):
        return pltpu.make_async_remote_copy(
            src_ref=src, dst_ref=dst, send_sem=ss.at[n], recv_sem=rs.at[n],
            device_id=who, device_id_type=MESH)

    left, down, corner = (d, lf), (dn_d, j), (dn_d, lf)
    fwd = [
        remote(send_a.at[0], recv_a.at[0], 0, left),
        remote(send_a.at[1], recv_a.at[1], 1, left),
        remote(send_s.at[0], recv_s.at[0], 2, left),
        remote(send_s.at[1], recv_s.at[1], 3, down),
        remote(send_s.at[2], recv_s.at[2], 4, corner),
    ]
    right, above, far = (d, rt), (up_d, j), (up_d, rt)
    ret = [
        remote(back_a.at[0], home_a.at[0], 5, right),
        remote(back_a.at[1], home_a.at[1], 6, right),
        remote(back_s.at[0], home_s.at[0], 7, right),
        remote(back_s.at[1], home_s.at[1], 8, above),
        remote(back_s.at[2], home_s.at[2], 9, far),
    ]

    mod_cp.wait()

    def rows_of(units):
        return jnp.concatenate([x[g, r] for g, r in units], axis=0)

    def norm_units(units):
        for k in range(0, len(units), 2):
            v = norm_mod(rows_of(units[k:k + 2]), mod[0])
            nbuf[pl.ds(24 * k, 48)] = v.astype(BF)

    first = True
    for k, r0 in ((0, 3), (1, 9)):
        for c in loads[k]:
            c.wait()
        norm_units([(g, r) for g in range(2) for r in range(r0, r0 + 6)])
        if first:
            wcp[0].wait()
        t0 = dot(pa[...], nbuf[pl.ds(0, 144)])
        t1 = dot(pa[...], nbuf[pl.ds(144, 144)])
        send_a[k] = jnp.concatenate([t0[:72], t1[:72]], axis=0).astype(BF)
        if first:
            pl.semaphore_wait(barrier, 6)
        first = False
        fwd[k].start()
        own_a[k] = jnp.concatenate([t0[72:], t1[72:]], axis=0).astype(BF)
    wcp[1].wait()
    for k, r0 in ((3, 0), (2, 15)):
        for c in loads[k]:
            c.wait()
        norm_units([(g, r) for g in range(2) for r in range(r0, r0 + 3)])
        t = dot(pc[...], nbuf[pl.ds(0, 144)])
        if k == 3:
            send_s[2] = t[:80].astype(BF)
            fwd[4].start()
            send_s[1] = t[80:].astype(BF)
            fwd[3].start()
        else:
            send_s[0] = t[:80].astype(BF)
            fwd[2].start()
            own_c[...] = t[80:].astype(BF)

    scale = math.log2(math.e) / math.sqrt(D // HEADS)
    lane = lax.broadcasted_iota(jnp.int32, (1, 128), 1)

    def attend(g, n, get_bias):
        def step(i, carry):
            col = pl.multiple_of(i * 128, 128)
            q = qkv[g, pl.ds(0, n), pl.ds(col, 128)]
            kk = qkv[g, pl.ds(0, n), pl.ds(512 + col, 128)]
            v = qkv[g, pl.ds(0, n), pl.ds(1024 + col, 128)]
            acc = None
            for h in range(4):
                inside = (lane >= 32 * h) & (lane < 32 * h + 32)
                qh = q * inside.astype(F32).astype(BF)
                s = lax.dot_general(qh, kk, (((1,), (1,)), ((), ())), preferred_element_type=F32)
                if get_bias is not None:
                    s = s + get_bias()
                p = jnp.exp2(s - jnp.max(s, axis=-1, keepdims=True))
                p = p * (1.0 / jnp.sum(p, axis=-1, keepdims=True))
                o = dot(p.astype(BF), v)
                acc = o if acc is None else jnp.where(inside, o, acc)
            ctx[g, pl.ds(0, n), pl.ds(col, 128)] = acc
            return carry

        lax.fori_loop(0, 4, step, 0)

    wcp[2].wait()
    wcp[3].wait()
    wcp[4].wait()

    def project_in(tokens, cut):
        parts = len(tokens)
        n = parts * cut
        rows = jnp.concatenate(tokens, axis=0)
        for c in range(3):
            y = dot(rows, wqkv[:, c * D:(c + 1) * D])
            if c == 0:
                y = y * scale
            for g in range(2):
                qkv[g, pl.ds(0, n), pl.ds(c * D, D)] = jnp.concatenate(
                    [y[2 * cut * m + g * cut:2 * cut * m + (g + 1) * cut] for m in range(parts)],
                    axis=0).astype(BF)

    for k in range(2):
        fwd[k].wait_recv()
        project_in([own_a[k], recv_a[k]], 72)
        attend(0, 144, None)
        attend(1, 144, lambda: bias[...])
        back_a[k] = jnp.concatenate(
            [ctx[0, pl.ds(72, 72)], ctx[1, pl.ds(72, 72)]], axis=0).astype(BF)
        ret[k].start()
        keep_a[k] = jnp.concatenate(
            [ctx[0, pl.ds(0, 72)], ctx[1, pl.ds(0, 72)]], axis=0).astype(BF)
    for n in (2, 3, 4):
        fwd[n].wait_recv()
    project_in([own_c[...], recv_s[0], recv_s[1], recv_s[2]], 40)
    last = lax.select(d == nlat - 1, 2, 0)
    attend(0, 160, lambda: bias_s[last])
    attend(1, 160, lambda: bias_s[last + 1])
    for m in (2, 1, 0):
        back_s[m] = jnp.concatenate(
            [ctx[0, pl.ds(40 + 40 * m, 40)], ctx[1, pl.ds(40 + 40 * m, 40)]], axis=0).astype(BF)
        ret[2 + m].start()
    keep_c[...] = jnp.concatenate(
        [ctx[0, pl.ds(0, 40)], ctx[1, pl.ds(0, 40)]], axis=0).astype(BF)

    for n in range(5, 10):
        wcp[n].wait()
    outs = []

    def finish(units, c_all, inv):
        at_home = dot(inv, c_all).astype(BF)
        attn = dot(at_home, wproj[...])
        for k in range(0, 12, 2):
            mid = rows_of(units[k:k + 2]) + attn[24 * k:24 * k + 48]
            for m in range(2):
                g, r = units[k + m]
                x[g, r] = mid[24 * m:24 * m + 24]
            n2[pl.ds(24 * k, 48)] = norm_mod(mid, mod[1]).astype(BF)
        total = None
        for c in range(FFH // HID):
            u = dot(n2[...], wup[:, c * HID:(c + 1) * HID])
            part = dot(gelu(u).astype(BF), wdown[c * HID:(c + 1) * HID])
            total = part if total is None else total + part
        for k, (g, r) in enumerate(units):
            x[g, r] = x[g, r] + total[24 * k:24 * k + 24]

    def write(k):
        r0, n = classes[k]
        for g in range(2):
            for s in range(2):
                lev = LEV[g][s]
                outs.append(pltpu.make_async_copy(
                    x.at[g, pl.ds(r0, n), pl.ds(8 * s, 8)],
                    out_hbm.at[lev, pl.ds(r0, n), pl.ds(0, 8)], out_sem.at[k, g, s, 0]))
                outs.append(pltpu.make_async_copy(
                    x.at[g, pl.ds(r0, n), pl.ds(16 + 4 * s, 4)],
                    out_hbm.at[lev, pl.ds(r0, n), pl.ds(8, 4)], out_sem.at[k, g, s, 1]))
        for c in outs[-8:]:
            c.start()

    for k, r0 in ((0, 3), (1, 9)):
        ret[k].wait_recv()
        finish([(g, r) for g in range(2) for r in range(r0, r0 + 6)],
               jnp.concatenate([keep_a[k], home_a[k]], axis=0), ia[...])
        write(k)
    for n in (2, 3, 4):
        ret[n].wait_recv()
    finish([(g, r) for r0 in (15, 0) for g in range(2) for r in range(r0, r0 + 3)],
           jnp.concatenate([keep_c[...], home_s[0], home_s[1], home_s[2]], axis=0), ic[...])
    write(2)
    write(3)
    for c in outs:
        c.wait()
    for c in fwd + ret:
        c.wait_send()


def solution(mesh):
    nlat, nlon = mesh.shape["lat"], mesh.shape["lon"]

    def local(latents, qkv_weight, proj_weight, up_weight, down_weight, modulation):
        consts = tables()
        vm = pltpu.VMEM
        scratch = [
            vm((2, 18, 24, D), F32), vm((D, 3 * D), BF), vm((D, D), BF), vm((D, FFH), BF),
            vm((FFH, D), BF), vm((2, 2, D), F32),
            *[vm(c.shape, BF if c.dtype == jnp.bfloat16 else F32) for c in consts],
            vm((288, D), BF), vm((2, 144, D), BF), vm((3, 80, D), BF), vm((2, 144, D), BF),
            vm((80, D), BF), vm((2, 144, D), BF), vm((3, 80, D), BF),
            vm((2, 160, 3 * D), BF), vm((2, 160, D), F32), vm((2, 144, D), BF), vm((80, D), BF),
            vm((2, 144, D), BF), vm((3, 80, D), BF), vm((2, 144, D), BF), vm((3, 80, D), BF),
            vm((288, D), BF),
            pltpu.SemaphoreType.DMA((4, 2, 2, 2)), pltpu.SemaphoreType.DMA((11,)),
            pltpu.SemaphoreType.DMA((4, 2, 2, 2)), pltpu.SemaphoreType.DMA((10,)),
            pltpu.SemaphoreType.DMA((10,)),
        ]
        return pl.pallas_call(
            functools.partial(kernel, nlat, nlon),
            out_shape=jax.ShapeDtypeStruct(latents.shape, F32),
            in_specs=[pl.BlockSpec(memory_space=pl.ANY)] * (6 + len(consts)),
            out_specs=pl.BlockSpec(memory_space=pl.ANY),
            scratch_shapes=scratch,
            compiler_params=pltpu.CompilerParams(
                collective_id=0, has_side_effects=True, vmem_limit_bytes=48 << 20),
        )(latents, qkv_weight, proj_weight, up_weight, down_weight, modulation,
          *[jnp.asarray(c) for c in consts])

    placed = (P(None, "lat", "lon", None), P(), P(), P(), P(), P())
    return jax.shard_map(
        local, mesh=mesh, in_specs=placed, out_specs=P(None, "lat", "lon", None), check_vma=False)
```

```python
import functools
import math

import jax
import jax.numpy as jnp
import numpy as np
from jax import lax
from jax.experimental import pallas as pl
from jax.experimental.pallas import tpu as pltpu
from jax.sharding import PartitionSpec as P

HEADS = 16
D = 512
FFH = 2048
UNROLL = 4
HID = 512
NEG = -1e30
BF = jnp.bfloat16
F32 = jnp.float32
MESH = pl.DeviceIdType.MESH
SLOT = {1: 0, 2: 1, 3: 2, 0: 3}
CLASSES = ((3, 6), (9, 6), (15, 3), (0, 3))


@functools.cache
def tables():
    pa = np.zeros((96, 96), np.float32)
    count = [0] * 4
    for h in range(2):
        for i in range(12):
            for lev in range(4):
                slot = SLOT[lev]
                pa[slot * 24 + count[slot], h * 48 + i * 4 + lev] = 1
                count[slot] += 1
    ps = np.zeros((288, 320), np.float32)
    count = [0] * 4
    for piece in range(4):
        for i in range(18):
            for lev in range(4):
                slot = SLOT[lev]
                ps[slot * 72 + count[slot], piece * 80 + i * 4 + lev] = 1
                count[slot] += 1
    bf = jnp.bfloat16
    return pa.astype(bf), pa.T.astype(bf), ps.astype(bf), ps.T.astype(bf)


def dot(a, b):
    return jnp.dot(a, b, preferred_element_type=F32)


def norm_mod(v, mod):
    mean = jnp.sum(v, axis=-1, keepdims=True) * (1.0 / D)
    c = v - mean
    var = jnp.sum(c * c, axis=-1, keepdims=True) * (1.0 / D)
    return (c * lax.rsqrt(var + 1e-5)) * (1.0 + mod[0:1]) + mod[1:2]


def gelu(u):
    return 0.5 * u * (1.0 + lax.erf(u * (1.0 / math.sqrt(2.0))))


def kernel(
    nlat, nlon,
    lat_hbm, wqkv_hbm, wproj_hbm, wup_hbm, wdown_hbm, mod_hbm,
    pa_hbm, pat_hbm, ps_hbm, pst_hbm,
    out_hbm,
    x, wqkv, wproj, wup, wdown, mod, pa, pat, ps, pst,
    send_a, send_s, own_a, own_c, recv_a, recv_s,
    qkv0, q1, kv1, ctx, keep_a, keep_c, back_a, back_s, home_a, home_s, n2,
    in_sem, w_sem, out_sem, ss, rs,
):
    d, j = lax.axis_index("lat"), lax.axis_index("lon")
    up_d, dn_d = lax.rem(d + 1, nlat), lax.rem(d + nlat - 1, nlat)
    rt, lf = lax.rem(j + 1, nlon), lax.rem(j + nlon - 1, nlon)
    barrier = pltpu.get_barrier_semaphore()
    for who in ((d, rt), (d, lf), (up_d, j), (dn_d, j), (up_d, rt), (dn_d, lf)):
        pl.semaphore_signal(barrier, inc=1, device_id=who, device_id_type=MESH)

    mod_cp = pltpu.make_async_copy(mod_hbm, mod, w_sem.at[0])
    mod_cp.start()
    near, far = 1 - lax.rem(j, 2), lax.rem(j, 2)

    def load(k, r0, n):
        return [pltpu.make_async_copy(
            lat_hbm.at[pl.ds(r0, n), :, p], x.at[pl.ds(r0, n), :, pl.ds(4 * p, 4)],
            in_sem.at[k, p]) for p in range(2)]

    loads = [load(far, 3 + 6 * far, 6), load(near, 3 + 6 * near, 6), load(2, 15, 3), load(3, 0, 3)]
    for cs in loads:
        for c in cs:
            c.start()
    wcp = []
    for i, (a, b) in enumerate((
        (pa_hbm, pa), (wqkv_hbm, wqkv), (pat_hbm, pat), (ps_hbm, ps), (pst_hbm, pst),
        (wproj_hbm, wproj), (wup_hbm, wup), (wdown_hbm, wdown),
    )):
        wcp.append(pltpu.make_async_copy(a, b, w_sem.at[i + 1]))
        wcp[-1].start()

    def remote(src, dst, n, who):
        return pltpu.make_async_remote_copy(
            src_ref=src, dst_ref=dst, send_sem=ss.at[n], recv_sem=rs.at[n],
            device_id=who, device_id_type=MESH)

    left, down, corner = (d, lf), (dn_d, j), (dn_d, lf)
    right, above, across = (d, rt), (up_d, j), (up_d, rt)

    def fwd_pair(k):
        return remote(send_a.at[k], recv_a.at[k], k, (d, jnp.where(k == 0, lf, rt)))

    def ret_pair(k):
        return remote(back_a.at[k], home_a.at[k], 5 + k, (d, jnp.where(k == 0, rt, lf)))

    fwd = [
        remote(send_s.at[0], recv_s.at[0], 2, left),
        remote(send_s.at[1], recv_s.at[1], 3, down),
        remote(send_s.at[2], recv_s.at[2], 4, corner),
    ]
    ret = [
        remote(back_s.at[0], home_s.at[0], 7, right),
        remote(back_s.at[1], home_s.at[1], 8, above),
        remote(back_s.at[2], home_s.at[2], 9, across),
    ]

    mod_cp.wait()

    def part(r, h):
        return x[r, pl.ds(3 * h, 3)].reshape(24, D)

    def norm_parts(rows, h):
        v = norm_mod(jnp.concatenate([part(r, h) for r in rows], axis=0), mod[0])
        if len(rows) == 3:
            v = jnp.concatenate([v, jnp.zeros((8, D), F32)], axis=0)
        return v.astype(BF)

    def fill(dst, k, h):
        for m in range(3):
            r = 3 + 6 * k + 2 * m
            dst[k, pl.ds(48 * m, 48)] = norm_parts((r, r + 1), h)

    for k, cs in ((far, loads[0]), (near, loads[1])):
        for c in cs:
            c.wait()
        fill(send_a, k, k)
        if k is far:
            pl.semaphore_wait(barrier, 6)
        fwd_pair(k).start()
    fill(own_a, far, near)
    for c in loads[3]:
        c.wait()
    send_s[2] = norm_parts((0, 1, 2), 0)
    fwd[2].start()
    send_s[1] = norm_parts((0, 1, 2), 1)
    fwd[1].start()
    for c in loads[2]:
        c.wait()
    send_s[0] = norm_parts((15, 16, 17), 0)
    fwd[0].start()
    own_c[...] = norm_parts((15, 16, 17), 1)
    fill(own_a, near, far)

    scale = math.log2(math.e) / math.sqrt(D // HEADS)
    lane = lax.broadcasted_iota(jnp.int32, (1, 128), 1)
    inside = [(lane >= 32 * h) & (lane < 32 * h + 32) for h in range(4)]
    cut = jnp.where(d == nlat - 1, NEG, 0.0)

    def apart(n):
        a = lax.rem(lax.broadcasted_iota(jnp.int32, (n, n), 0), 72) < 36
        b = lax.rem(lax.broadcasted_iota(jnp.int32, (n, n), 1), 72) < 36
        return jnp.where(a != b, cut, 0.0)

    def heads(q, kk, v, bias):
        n = kk.shape[0]
        q4 = jnp.concatenate([q * inside[h].astype(F32).astype(q.dtype) for h in range(4)], axis=0)
        s4 = lax.dot_general(q4.astype(BF), kk, (((1,), (1,)), ((), ())), preferred_element_type=F32)
        p4 = []
        for h in range(4):
            s = s4[n * h:n * h + n]
            if bias is not None:
                s = s + bias
            p4.append(jnp.exp2(s - jnp.max(s, axis=-1, keepdims=True)))
        o4 = dot(jnp.concatenate(p4, axis=0).astype(BF),
                 jnp.concatenate([v, jnp.ones((n, 128), BF)], axis=1))
        top, low = o4[:n, :128], o4[:n, 128:]
        for h in range(1, 4):
            top = jnp.where(inside[h], o4[n * h:n * h + n, :128], top)
            low = jnp.where(inside[h], o4[n * h:n * h + n, 128:], low)
        return top * (1.0 / low)

    def attend(masked):
        def step(i, carry):
            cols = [pl.ds(pl.multiple_of(512 * m + i * 128, 128), 128) for m in range(3)]
            ctx[pl.ds(0, 144), cols[0]] = heads(
                *[qkv0[:, c] for c in cols], apart(144) if masked else None)
            for m in range(2):
                ctx[pl.ds(144 + 72 * m, 72), cols[0]] = heads(
                    q1[pl.ds(72 * m, 72), cols[0]], *[kv1[m, pl.ds(0, 72), c] for c in cols[:2]],
                    apart(72) if masked else None)
            return carry

        lax.fori_loop(0, 4, step, 0, unroll=UNROLL)

    def project_in(rows):
        for c in range(3):
            cols = slice(c * D, (c + 1) * D)
            y = dot(rows, wqkv[:, cols])
            if c == 0:
                y = y * scale
            qkv0[:, cols] = y[:144].astype(BF)
            if c == 0:
                q1[...] = y[144:]
            else:
                for m in range(2):
                    kv1[m, pl.ds(0, 72), slice((c - 1) * D, c * D)] = y[144 + 72 * m:216 + 72 * m].astype(BF)

    wcp[0].wait()
    wcp[1].wait()
    for k in (far, near):
        fwd_pair(k).wait_recv()
        t = [dot(pa[...], jnp.concatenate(
            [own_a[k, pl.ds(48 * m, 48)], recv_a[k, pl.ds(48 * m, 48)]], axis=0)) for m in range(3)]
        project_in(jnp.concatenate(
            [t[m][24 * s:24 * s + 24] for s in range(4) for m in range(3)], axis=0).astype(BF))
        attend(False)
        if k is far:
            wcp[2].wait()
        for m in range(3):
            t = dot(pat[...], jnp.concatenate(
                [ctx[pl.ds(72 * s + 24 * m, 24)] for s in range(4)], axis=0).astype(BF))
            keep_a[k, pl.ds(48 * m, 48)] = t[:48].astype(BF)
            back_a[k, pl.ds(48 * m, 48)] = t[48:].astype(BF)
        ret_pair(k).start()
    for c in fwd:
        c.wait_recv()
    wcp[3].wait()
    wcp[4].wait()
    project_in(dot(ps[...], jnp.concatenate(
        [own_c[...], recv_s[0], recv_s[1], recv_s[2]], axis=0)).astype(BF))
    attend(True)
    t = dot(pst[...], ctx[...].astype(BF))
    for m in (2, 1, 0):
        back_s[m] = t[80 * m + 80:80 * m + 160].astype(BF)
        ret[m].start()
    keep_c[...] = t[:80].astype(BF)

    for n in range(5, 8):
        wcp[n].wait()
    outs = []

    def finish(pieces, context):
        attn = dot(context, wproj[...])
        for k in range(0, 12, 2):
            mid = jnp.concatenate([part(r, h) + attn[o:o + 24] for r, h, o in pieces[k:k + 2]], axis=0)
            for m in range(2):
                r, h, _ = pieces[k + m]
                x[r, pl.ds(3 * h, 3)] = mid[24 * m:24 * m + 24].reshape(3, 8, D)
            n2[pl.ds(24 * k, 48)] = norm_mod(mid, mod[1]).astype(BF)
        total = None
        for c in range(FFH // HID):
            u = dot(n2[...], wup[:, c * HID:(c + 1) * HID])
            more = dot(gelu(u).astype(BF), wdown[c * HID:(c + 1) * HID])
            total = more if total is None else total + more
        for k, (r, h, _) in enumerate(pieces):
            x[r, pl.ds(3 * h, 3)] = (part(r, h) + total[24 * k:24 * k + 24]).reshape(3, 8, D)

    def write(k, r0, n):
        for p in range(2):
            outs.append(pltpu.make_async_copy(
                x.at[pl.ds(r0, n), :, pl.ds(4 * p, 4)], out_hbm.at[pl.ds(r0, n), :, p],
                out_sem.at[k, p]))
            outs[-1].start()

    for k in (near, far):
        ret_pair(k).wait_recv()
        r0 = 3 + 6 * k
        finish([(r0 + i, h, o + 24 * i) for h, o in ((k, 0), (1 - k, 144)) for i in range(6)],
               jnp.concatenate([home_a[k], keep_a[k]], axis=0))
        write(k, r0, 6)
    for c in ret:
        c.wait_recv()
    finish([(r0 + i, h, o + 24 * i) for r0, h, o in ((15, 1, 0), (15, 0, 80), (0, 1, 160), (0, 0, 240))
            for i in range(3)],
           jnp.concatenate([keep_c[...], home_s[0], home_s[1], home_s[2]], axis=0))
    write(2, 15, 3)
    write(3, 0, 3)
    for c in outs:
        c.wait()
    for c in [fwd_pair(0), fwd_pair(1), ret_pair(0), ret_pair(1)] + fwd + ret:
        c.wait_send()


def hand_over(a, b, buf, sems):
    steps = [pl.ds(3 * i, 3) for i in range(6)]
    first = [pltpu.make_async_copy(a.at[t], buf.at[t], sems.at[0, i]) for i, t in enumerate(steps)]
    second = [pltpu.make_async_copy(buf.at[t], b.at[t], sems.at[1, i]) for i, t in enumerate(steps)]
    for c in first:
        c.start()
    for c, e in zip(first, second):
        c.wait()
        e.start()
    for e in second:
        e.wait()


def solution(mesh):
    nlat, nlon = mesh.shape["lat"], mesh.shape["lon"]

    def local(latents, qkv_weight, proj_weight, up_weight, down_weight, modulation):
        consts = tables()
        vm = pltpu.VMEM
        view = latents.transpose(1, 2, 0, 3).reshape(18, 6, 2, 4, D)
        scratch = [
            vm((18, 6, 8, D), F32), vm((D, 3 * D), BF), vm((D, D), BF), vm((D, FFH), BF),
            vm((FFH, D), BF), vm((2, 2, D), F32),
            *[vm(c.shape, BF) for c in consts],
            vm((2, 144, D), BF), vm((3, 80, D), BF), vm((2, 144, D), BF),
            vm((80, D), BF), vm((2, 144, D), BF), vm((3, 80, D), BF),
            vm((144, 3 * D), BF), vm((144, D), F32), vm((2, 80, 2 * D), BF), vm((288, D), F32), vm((2, 144, D), BF),
            vm((80, D), BF),
            vm((2, 144, D), BF), vm((3, 80, D), BF), vm((2, 144, D), BF), vm((3, 80, D), BF),
            vm((288, D), BF),
            pltpu.SemaphoreType.DMA((4, 2)), pltpu.SemaphoreType.DMA((9,)),
            pltpu.SemaphoreType.DMA((4, 2)), pltpu.SemaphoreType.DMA((10,)),
            pltpu.SemaphoreType.DMA((10,)),
        ]
        out = pl.pallas_call(
            functools.partial(kernel, nlat, nlon),
            out_shape=jax.ShapeDtypeStruct(view.shape, F32),
            in_specs=[pl.BlockSpec(memory_space=pl.ANY)] * (6 + len(consts)),
            out_specs=pl.BlockSpec(memory_space=pl.ANY),
            scratch_shapes=scratch,
            compiler_params=pltpu.CompilerParams(
                collective_id=0, has_side_effects=True, vmem_limit_bytes=62 << 20),
        )(view, qkv_weight, proj_weight, up_weight, down_weight, modulation,
          *[jnp.asarray(c) for c in consts])
        out = pl.pallas_call(
            hand_over,
            out_shape=jax.ShapeDtypeStruct(view.shape, F32),
            in_specs=[pl.BlockSpec(memory_space=pl.ANY)],
            out_specs=pl.BlockSpec(memory_space=pl.ANY),
            scratch_shapes=[vm(view.shape, F32), pltpu.SemaphoreType.DMA((2, 6))],
            compiler_params=pltpu.CompilerParams(vmem_limit_bytes=62 << 20),
        )(out)
        return out.reshape(18, 12, 4, D).transpose(2, 0, 1, 3)

    placed = (P(None, "lat", "lon", None), P(), P(), P(), P(), P())
    return jax.shard_map(
        local, mesh=mesh, in_specs=placed, out_specs=P(None, "lat", "lon", None), check_vma=False)
```

```python
import functools
import math

import jax
import jax.numpy as jnp
import numpy as np
from jax import lax
from jax.experimental import pallas as pl
from jax.experimental.pallas import tpu as pltpu
from jax.sharding import PartitionSpec as P

HEADS = 16
D = 512
FFH = 2048
UNROLL = 4
VM = 60
HID = 512
NEG = -1e30
BF = jnp.bfloat16
F32 = jnp.float32
MESH = pl.DeviceIdType.MESH
SLOT = {1: 0, 2: 1, 3: 2, 0: 3}
CLASSES = ((3, 6), (9, 6), (15, 3), (0, 3))


@functools.cache
def tables():
    pa = np.zeros((96, 96), np.float32)
    count = [0] * 4
    for h in range(2):
        for i in range(12):
            for lev in range(4):
                slot = SLOT[lev]
                pa[slot * 24 + count[slot], h * 48 + i * 4 + lev] = 1
                count[slot] += 1
    ps = np.zeros((288, 320), np.float32)
    count = [0] * 4
    for piece in range(4):
        for i in range(18):
            for lev in range(4):
                slot = SLOT[lev]
                ps[slot * 72 + count[slot], piece * 80 + i * 4 + lev] = 1
                count[slot] += 1
    bf = jnp.bfloat16
    return pa.astype(bf), pa.T.astype(bf), ps.astype(bf), ps.T.astype(bf)


def dot(a, b):
    return jnp.dot(a, b, preferred_element_type=F32)


def norm_mod(v, mod):
    mean = jnp.sum(v, axis=-1, keepdims=True) * (1.0 / D)
    c = v - mean
    var = jnp.sum(c * c, axis=-1, keepdims=True) * (1.0 / D)
    return (c * lax.rsqrt(var + 1e-5)) * (1.0 + mod[0:1]) + mod[1:2]


def gelu(u):
    return 0.5 * u * (1.0 + lax.erf(u * (1.0 / math.sqrt(2.0))))


def kernel(
    nlat, nlon,
    lat_hbm, wqkv_hbm, wproj_hbm, wup_hbm, wdown_hbm, mod_hbm,
    pa_hbm, pat_hbm, ps_hbm, pst_hbm,
    x,
    wqkv, wproj, wup, wdown, mod, pa, pat, ps, pst,
    send_a, send_s, own_a, own_c, recv_a, recv_s,
    qkv0, q1, kv1, ctx, keep_a, keep_c, back_a, back_s, home_a, home_s, n2,
    in_sem, w_sem, ss, rs,
):
    d, j = lax.axis_index("lat"), lax.axis_index("lon")
    up_d, dn_d = lax.rem(d + 1, nlat), lax.rem(d + nlat - 1, nlat)
    rt, lf = lax.rem(j + 1, nlon), lax.rem(j + nlon - 1, nlon)
    barrier = pltpu.get_barrier_semaphore()
    for who in ((d, rt), (d, lf), (up_d, j), (dn_d, j), (up_d, lf), (dn_d, rt)):
        pl.semaphore_signal(barrier, inc=1, device_id=who, device_id_type=MESH)

    mod_cp = pltpu.make_async_copy(mod_hbm, mod, w_sem.at[0])
    mod_cp.start()
    near, far = 1 - lax.rem(j, 2), lax.rem(j, 2)

    def load(n, r0, count, h):
        return [pltpu.make_async_copy(
            lat_hbm.at[pl.ds(r0, count), pl.ds(3 * h, 3), p],
            x.at[pl.ds(r0, count), pl.ds(3 * h, 3), pl.ds(4 * p, 4)], in_sem.at[n, p]) for p in range(2)]

    loads = [load(0, 3 + 6 * far, 6, far), load(1, 3 + 6 * near, 6, near), load(2, 3 + 6 * far, 6, near),
             load(3, 3 + 6 * near, 6, far), load(4, 15, 3, 0), load(5, 15, 3, 1), load(6, 0, 3, 0), load(7, 0, 3, 1)]
    for cs in loads:
        for c in cs:
            c.start()
    wcp = []
    for i, (a, b) in enumerate((
        (pa_hbm, pa), (wqkv_hbm, wqkv), (pat_hbm, pat), (ps_hbm, ps), (pst_hbm, pst),
        (wproj_hbm, wproj), (wup_hbm, wup), (wdown_hbm, wdown),
    )):
        wcp.append(pltpu.make_async_copy(a, b, w_sem.at[i + 1]))
        wcp[-1].start()

    def remote(src, dst, n, who):
        return pltpu.make_async_remote_copy(
            src_ref=src, dst_ref=dst, send_sem=ss.at[n], recv_sem=rs.at[n],
            device_id=who, device_id_type=MESH)

    right, left, down, above = (d, rt), (d, lf), (dn_d, j), (up_d, j)

    def fwd_pair(k):
        return remote(send_a.at[k], recv_a.at[k], k, (d, jnp.where(k == 0, lf, rt)))

    def ret_pair(k):
        return remote(back_a.at[k], home_a.at[k], 5 + k, (d, jnp.where(k == 0, rt, lf)))

    fwd = [
        remote(send_s.at[0], recv_s.at[0], 2, right),
        remote(send_s.at[1], recv_s.at[1], 3, down),
        remote(send_s.at[2], recv_s.at[2], 4, (dn_d, rt)),
    ]
    ret = [
        remote(back_s.at[0], home_s.at[0], 7, left),
        remote(back_s.at[1], home_s.at[1], 8, above),
        remote(back_s.at[2], home_s.at[2], 9, (up_d, lf)),
    ]

    mod_cp.wait()

    def part(r, h):
        return x[r, pl.ds(3 * h, 3)].reshape(24, D)

    def norm_parts(rows, h):
        v = norm_mod(jnp.concatenate([part(r, h) for r in rows], axis=0), mod[0])
        if len(rows) == 3:
            v = jnp.concatenate([v, jnp.zeros((8, D), F32)], axis=0)
        return v.astype(BF)

    def fill(dst, k, h):
        for m in range(3):
            r = 3 + 6 * k + 2 * m
            dst[k, pl.ds(48 * m, 48)] = norm_parts((r, r + 1), h)

    for k, cs in ((far, loads[0]), (near, loads[1])):
        for c in cs:
            c.wait()
        fill(send_a, k, k)
        if k is far:
            pl.semaphore_wait(barrier, 6)
        fwd_pair(k).start()
    for c in loads[2]:
        c.wait()
    fill(own_a, far, near)

    def send_rest():
        for cs in loads[3:]:
            for c in cs:
                c.wait()
        send_s[2] = norm_parts((0, 1, 2), 1)
        send_s[1] = norm_parts((0, 1, 2), 0)
        send_s[0] = norm_parts((15, 16, 17), 1)

    send_rest()

    scale = math.log2(math.e) / math.sqrt(D // HEADS)
    lane = lax.broadcasted_iota(jnp.int32, (1, 128), 1)
    inside = [(lane >= 32 * h) & (lane < 32 * h + 32) for h in range(4)]
    cut = jnp.where(d == nlat - 1, NEG, 0.0)

    def apart(n):
        a = lax.rem(lax.broadcasted_iota(jnp.int32, (n, n), 0), 72) < 36
        b = lax.rem(lax.broadcasted_iota(jnp.int32, (n, n), 1), 72) < 36
        return jnp.where(a != b, cut, 0.0)

    def heads(q, kk, v, bias):
        n = kk.shape[0]
        q4 = jnp.concatenate([q * inside[h].astype(F32).astype(q.dtype) for h in range(4)], axis=0)
        s4 = lax.dot_general(q4.astype(BF), kk, (((1,), (1,)), ((), ())), preferred_element_type=F32)
        p4 = []
        for h in range(4):
            s = s4[n * h:n * h + n]
            if bias is not None:
                s = s + bias
            p4.append(jnp.exp2(s - jnp.max(s, axis=-1, keepdims=True)))
        o4 = dot(jnp.concatenate(p4, axis=0).astype(BF),
                 jnp.concatenate([v, jnp.ones((n, 128), BF)], axis=1))
        top, low = o4[:n, :128], o4[:n, 128:]
        for h in range(1, 4):
            top = jnp.where(inside[h], o4[n * h:n * h + n, :128], top)
            low = jnp.where(inside[h], o4[n * h:n * h + n, 128:], low)
        return top * (1.0 / low)

    def attend(masked):
        def step(i, carry):
            cols = [pl.ds(pl.multiple_of(512 * m + i * 128, 128), 128) for m in range(3)]
            ctx[pl.ds(0, 144), cols[0]] = heads(
                *[qkv0[:, c] for c in cols], apart(144) if masked else None)
            for m in range(2):
                ctx[pl.ds(144 + 72 * m, 72), cols[0]] = heads(
                    q1[pl.ds(72 * m, 72), cols[0]], *[kv1[m, pl.ds(0, 72), c] for c in cols[:2]],
                    apart(72) if masked else None)
            return carry

        lax.fori_loop(0, 4, step, 0, unroll=UNROLL)

    def project_in(rows):
        for c in range(3):
            cols = slice(c * D, (c + 1) * D)
            y = dot(rows, wqkv[:, cols])
            if c == 0:
                y = y * scale
            qkv0[:, cols] = y[:144].astype(BF)
            if c == 0:
                q1[...] = y[144:]
            else:
                for m in range(2):
                    kv1[m, pl.ds(0, 72), slice((c - 1) * D, c * D)] = y[144 + 72 * m:216 + 72 * m].astype(BF)


    def finish(pieces, context):
        attn = dot(context, wproj[...])
        count = len(pieces)
        for k in range(0, count, 2):
            pair = pieces[k:k + 2]
            mid = jnp.concatenate([part(r, h) + attn[o:o + 24] for r, h, o in pair], axis=0)
            for m, (r, h, _) in enumerate(pair):
                x[r, pl.ds(3 * h, 3)] = mid[24 * m:24 * m + 24].reshape(3, 8, D)
            v = norm_mod(mid, mod[1])
            if len(pair) == 1:
                v = jnp.concatenate([v, jnp.zeros((8, D), F32)], axis=0)
            n2[pl.ds(24 * k, v.shape[0])] = v.astype(BF)
        rows = pl.ds(0, 24 * count + 8 * (count % 2))
        total = None
        for c in range(FFH // HID):
            u = dot(n2[rows], wup[:, c * HID:(c + 1) * HID])
            more = dot(gelu(u).astype(BF), wdown[c * HID:(c + 1) * HID])
            total = more if total is None else total + more
        for k, (r, h, _) in enumerate(pieces):
            x[r, pl.ds(3 * h, 3)] = (part(r, h) + total[24 * k:24 * k + 24]).reshape(3, 8, D)

    def span(k, h, o):
        return [(3 + 6 * k + i, h, o + 24 * i) for i in range(6)]

    wcp[0].wait()
    wcp[1].wait()
    for k in (far, near):
        fwd_pair(k).wait_recv()
        t = [dot(pa[...], jnp.concatenate(
            [own_a[k, pl.ds(48 * m, 48)], recv_a[k, pl.ds(48 * m, 48)]], axis=0)) for m in range(3)]
        project_in(jnp.concatenate(
            [t[m][24 * s:24 * s + 24] for s in range(4) for m in range(3)], axis=0).astype(BF))
        attend(False)
        if k is far:
            for c in (fwd[2], fwd[1], fwd[0]):
                c.start()
        if k is far:
            wcp[2].wait()
        for m in range(3):
            t = dot(pat[...], jnp.concatenate(
                [ctx[pl.ds(72 * s + 24 * m, 24)] for s in range(4)], axis=0).astype(BF))
            keep_a[k, pl.ds(48 * m, 48)] = t[:48].astype(BF)
            back_a[k, pl.ds(48 * m, 48)] = t[48:].astype(BF)
        ret_pair(k).start()
        if k is far:
            own_c[...] = norm_parts((15, 16, 17), 0)
            fill(own_a, near, far)
            for n in range(5, 8):
                wcp[n].wait()
            finish(span(far, near, 0), keep_a[far])
    for c in fwd:
        c.wait_recv()
    wcp[3].wait()
    wcp[4].wait()
    project_in(dot(ps[...], jnp.concatenate(
        [own_c[...], recv_s[0], recv_s[1], recv_s[2]], axis=0)).astype(BF))
    attend(True)
    t = dot(pst[...], ctx[...].astype(BF))
    for m in (2, 1, 0):
        back_s[m] = t[80 * m + 80:80 * m + 160].astype(BF)
        ret[m].start()
    keep_c[...] = t[:80].astype(BF)

    ret_pair(near).wait_recv()
    finish(span(near, near, 0) + span(near, far, 144), jnp.concatenate([home_a[near], keep_a[near]], axis=0))
    ret_pair(far).wait_recv()
    finish(span(far, far, 0) + [(15 + i, 0, 144 + 24 * i) for i in range(3)],
           jnp.concatenate([home_a[far], keep_c[...]], axis=0))
    for c in ret:
        c.wait_recv()
    finish([(r0 + i, h, o + 24 * i) for r0, h, o in ((15, 1, 0), (0, 0, 80), (0, 1, 160)) for i in range(3)],
           jnp.concatenate([home_s[0], home_s[1], home_s[2]], axis=0))
    for c in [fwd_pair(0), fwd_pair(1), ret_pair(0), ret_pair(1)] + fwd + ret:
        c.wait_send()


def hand_over(a, b, sems):
    copies = [pltpu.make_async_copy(
        a.at[pl.ds(3 * i, 3), :, pl.ds(4 * p, 4)], b.at[pl.ds(3 * i, 3), :, p], sems.at[i, p])
        for i in range(6) for p in range(2)]
    for c in copies:
        c.start()
    for c in copies:
        c.wait()


def solution(mesh):
    nlat, nlon = mesh.shape["lat"], mesh.shape["lon"]

    def local(latents, qkv_weight, proj_weight, up_weight, down_weight, modulation):
        consts = tables()
        vm = pltpu.VMEM
        view = latents.transpose(1, 2, 0, 3).reshape(18, 6, 2, 4, D)
        scratch = [
            vm((D, 3 * D), BF), vm((D, D), BF), vm((D, FFH), BF),
            vm((FFH, D), BF), vm((2, 2, D), F32),
            *[vm(c.shape, BF) for c in consts],
            vm((2, 144, D), BF), vm((3, 80, D), BF), vm((2, 144, D), BF),
            vm((80, D), BF), vm((2, 144, D), BF), vm((3, 80, D), BF),
            vm((144, 3 * D), BF), vm((144, D), F32), vm((2, 80, 2 * D), BF), vm((288, D), F32), vm((2, 144, D), BF),
            vm((80, D), BF),
            vm((2, 144, D), BF), vm((3, 80, D), BF), vm((2, 144, D), BF), vm((3, 80, D), BF),
            vm((288, D), BF),
            pltpu.SemaphoreType.DMA((8, 2)), pltpu.SemaphoreType.DMA((9,)),
            pltpu.SemaphoreType.DMA((10,)),
            pltpu.SemaphoreType.DMA((10,)),
        ]
        out = pl.pallas_call(
            functools.partial(kernel, nlat, nlon),
            out_shape=pltpu.VMEM((18, 6, 8, D), F32),
            in_specs=[pl.BlockSpec(memory_space=pl.ANY)] * (6 + len(consts)),
            out_specs=pl.BlockSpec(memory_space=pltpu.VMEM),
            scratch_shapes=scratch,
            compiler_params=pltpu.CompilerParams(
                collective_id=0, has_side_effects=True, vmem_limit_bytes=VM << 20),
        )(view, qkv_weight, proj_weight, up_weight, down_weight, modulation,
          *[jnp.asarray(c) for c in consts])
        out = pl.pallas_call(
            hand_over,
            out_shape=jax.ShapeDtypeStruct(view.shape, F32),
            in_specs=[pl.BlockSpec(memory_space=pltpu.VMEM)],
            out_specs=pl.BlockSpec(memory_space=pl.ANY),
            scratch_shapes=[pltpu.SemaphoreType.DMA((6, 2))],
            compiler_params=pltpu.CompilerParams(vmem_limit_bytes=16 << 20),
        )(out)
        return out.reshape(18, 12, 4, D).transpose(2, 0, 1, 3)

    placed = (P(None, "lat", "lon", None), P(), P(), P(), P(), P())
    return jax.shard_map(
        local, mesh=mesh, in_specs=placed, out_specs=P(None, "lat", "lon", None), check_vma=False)
```

```python
import functools
import math

import jax
import jax.numpy as jnp
import numpy as np
from jax import lax
from jax.experimental import pallas as pl
from jax.experimental.pallas import tpu as pltpu
from jax.sharding import PartitionSpec as P

HEADS = 16
D = 512
FFH = 2048
UNROLL = 4
VM = 60
HID = 512
NEG = -1e30
BF = jnp.bfloat16
F32 = jnp.float32
MESH = pl.DeviceIdType.MESH
SLOT = {1: 0, 2: 1, 3: 2, 0: 3}
CLASSES = ((3, 6), (9, 6), (15, 3), (0, 3))


@functools.cache
def tables():
    pa = np.zeros((96, 96), np.float32)
    count = [0] * 4
    for h in range(2):
        for i in range(12):
            for lev in range(4):
                slot = SLOT[lev]
                pa[slot * 24 + count[slot], h * 48 + i * 4 + lev] = 1
                count[slot] += 1
    ps = np.zeros((288, 320), np.float32)
    count = [0] * 4
    for piece in range(4):
        for i in range(18):
            for lev in range(4):
                slot = SLOT[lev]
                ps[slot * 72 + count[slot], piece * 80 + i * 4 + lev] = 1
                count[slot] += 1
    bf = jnp.bfloat16
    return pa.astype(bf), pa.T.astype(bf), ps.astype(bf), ps.T.astype(bf)


def dot(a, b):
    return jnp.dot(a, b, preferred_element_type=F32)


def norm_mod(v, mod):
    mean = jnp.sum(v, axis=-1, keepdims=True) * (1.0 / D)
    c = v - mean
    var = jnp.sum(c * c, axis=-1, keepdims=True) * (1.0 / D)
    return (c * lax.rsqrt(var + 1e-5)) * (1.0 + mod[0:1]) + mod[1:2]


def gelu(u):
    return 0.5 * u * (1.0 + lax.erf(u * (1.0 / math.sqrt(2.0))))


def kernel(
    nlat, nlon,
    lat_hbm, wqkv_hbm, wproj_hbm, wup_hbm, wdown_hbm, mod_hbm,
    pa_hbm, pat_hbm, ps_hbm, pst_hbm,
    x,
    wqkv, wproj, wup, wdown, mod, pa, pat, ps, pst,
    send_a, send_s, own_a, own_c, recv_a, recv_s,
    qkv0, q1, kv1, ctx, keep_a, keep_c, back_a, back_s, home_a, home_s, n2,
    in_sem, w_sem, ss, rs,
):
    d, j = lax.axis_index("lat"), lax.axis_index("lon")
    up_d, dn_d = lax.rem(d + 1, nlat), lax.rem(d + nlat - 1, nlat)
    rt, lf = lax.rem(j + 1, nlon), lax.rem(j + nlon - 1, nlon)
    barrier = pltpu.get_barrier_semaphore()
    for who in ((d, rt), (d, lf), (up_d, j), (dn_d, j), (up_d, lf), (dn_d, rt)):
        pl.semaphore_signal(barrier, inc=1, device_id=who, device_id_type=MESH)

    mod_cp = pltpu.make_async_copy(mod_hbm, mod, w_sem.at[0])
    mod_cp.start()
    near, far = 1 - lax.rem(j, 2), lax.rem(j, 2)

    def load(n, r0, count, h):
        return [pltpu.make_async_copy(
            lat_hbm.at[pl.ds(r0, count), pl.ds(3 * h, 3), p],
            x.at[pl.ds(r0, count), pl.ds(3 * h, 3), pl.ds(4 * p, 4)], in_sem.at[n, p]) for p in range(2)]

    loads = [load(0, 3 + 6 * far, 6, far), load(1, 3 + 6 * near, 6, near), load(2, 3 + 6 * far, 6, near),
             load(3, 3 + 6 * near, 6, far), load(4, 15, 3, 0), load(5, 15, 3, 1), load(6, 0, 3, 0), load(7, 0, 3, 1)]
    for cs in loads:
        for c in cs:
            c.start()
    wcp = []
    for i, (a, b) in enumerate((
        (pa_hbm, pa), (wqkv_hbm, wqkv), (pat_hbm, pat), (ps_hbm, ps), (pst_hbm, pst),
        (wproj_hbm, wproj), (wup_hbm, wup), (wdown_hbm, wdown),
    )):
        wcp.append(pltpu.make_async_copy(a, b, w_sem.at[i + 1]))
        wcp[-1].start()

    def remote(src, dst, n, who):
        return pltpu.make_async_remote_copy(
            src_ref=src, dst_ref=dst, send_sem=ss.at[n], recv_sem=rs.at[n],
            device_id=who, device_id_type=MESH)

    right, left, down, above = (d, rt), (d, lf), (dn_d, j), (up_d, j)

    def fwd_pair(k):
        return remote(send_a.at[k], recv_a.at[k], k, (d, jnp.where(k == 0, lf, rt)))

    def ret_pair(k):
        return remote(back_a.at[k], home_a.at[k], 5 + k, (d, jnp.where(k == 0, rt, lf)))

    fwd = [
        remote(send_s.at[0], recv_s.at[0], 2, right),
        remote(send_s.at[1], recv_s.at[1], 3, down),
        remote(send_s.at[2], recv_s.at[2], 4, (dn_d, rt)),
    ]
    ret = [
        remote(back_s.at[0], home_s.at[0], 7, left),
        remote(back_s.at[1], home_s.at[1], 8, above),
        remote(back_s.at[2], home_s.at[2], 9, (up_d, lf)),
    ]

    mod_cp.wait()

    def part(r, h):
        return x[r, pl.ds(3 * h, 3)].reshape(24, D)

    def norm_parts(rows, h):
        v = norm_mod(jnp.concatenate([part(r, h) for r in rows], axis=0), mod[0])
        if len(rows) == 3:
            v = jnp.concatenate([v, jnp.zeros((8, D), F32)], axis=0)
        return v.astype(BF)

    def fill(dst, k, h):
        for m in range(3):
            r = 3 + 6 * k + 2 * m
            dst[k, pl.ds(48 * m, 48)] = norm_parts((r, r + 1), h)

    for n, r0, h, dst in ((7, 0, 1, 2), (6, 0, 0, 1), (5, 15, 1, 0)):
        for c in loads[n]:
            c.wait()
        send_s[dst] = norm_parts((r0, r0 + 1, r0 + 2), h)
    pl.semaphore_wait(barrier, 6)
    for c in (fwd[2], fwd[1], fwd[0]):
        c.start()
    for c in loads[0]:
        c.wait()
    fill(send_a, far, far)
    fwd_pair(far).start()
    for c in loads[1]:
        c.wait()
    fill(send_a, near, near)
    fwd_pair(near).start()
    for c in loads[2]:
        c.wait()
    fill(own_a, far, near)

    scale = math.log2(math.e) / math.sqrt(D // HEADS)
    lane = lax.broadcasted_iota(jnp.int32, (1, 128), 1)
    inside = [(lane >= 32 * h) & (lane < 32 * h + 32) for h in range(4)]
    cut = jnp.where(d == nlat - 1, NEG, 0.0)

    def apart(n):
        a = lax.rem(lax.broadcasted_iota(jnp.int32, (n, n), 0), 72) < 36
        b = lax.rem(lax.broadcasted_iota(jnp.int32, (n, n), 1), 72) < 36
        return jnp.where(a != b, cut, 0.0)

    def heads(q, kk, v, bias):
        n = kk.shape[0]
        q4 = jnp.concatenate([q * inside[h].astype(F32).astype(q.dtype) for h in range(4)], axis=0)
        s4 = lax.dot_general(q4.astype(BF), kk, (((1,), (1,)), ((), ())), preferred_element_type=F32)
        p4 = []
        for h in range(4):
            s = s4[n * h:n * h + n]
            if bias is not None:
                s = s + bias
            p4.append(jnp.exp2(s - jnp.max(s, axis=-1, keepdims=True)))
        o4 = dot(jnp.concatenate(p4, axis=0).astype(BF),
                 jnp.concatenate([v, jnp.ones((n, 128), BF)], axis=1))
        top, low = o4[:n, :128], o4[:n, 128:]
        for h in range(1, 4):
            top = jnp.where(inside[h], o4[n * h:n * h + n, :128], top)
            low = jnp.where(inside[h], o4[n * h:n * h + n, 128:], low)
        return top * (1.0 / low)

    def attend(masked):
        def step(i, carry):
            cols = [pl.ds(pl.multiple_of(512 * m + i * 128, 128), 128) for m in range(3)]
            ctx[pl.ds(0, 144), cols[0]] = heads(
                *[qkv0[:, c] for c in cols], apart(144) if masked else None)
            for m in range(2):
                ctx[pl.ds(144 + 72 * m, 72), cols[0]] = heads(
                    q1[pl.ds(72 * m, 72), cols[0]], *[kv1[m, pl.ds(0, 72), c] for c in cols[:2]],
                    apart(72) if masked else None)
            return carry

        lax.fori_loop(0, 4, step, 0, unroll=UNROLL)

    def project_in(rows):
        for c in range(3):
            cols = slice(c * D, (c + 1) * D)
            y = dot(rows, wqkv[:, cols])
            if c == 0:
                y = y * scale
            qkv0[:, cols] = y[:144].astype(BF)
            if c == 0:
                q1[...] = y[144:]
            else:
                for m in range(2):
                    kv1[m, pl.ds(0, 72), slice((c - 1) * D, c * D)] = y[144 + 72 * m:216 + 72 * m].astype(BF)


    def finish(pieces, context):
        attn = dot(context, wproj[...])
        count = len(pieces)
        for k in range(0, count, 2):
            pair = pieces[k:k + 2]
            mid = jnp.concatenate([part(r, h) + attn[o:o + 24] for r, h, o in pair], axis=0)
            for m, (r, h, _) in enumerate(pair):
                x[r, pl.ds(3 * h, 3)] = mid[24 * m:24 * m + 24].reshape(3, 8, D)
            v = norm_mod(mid, mod[1])
            if len(pair) == 1:
                v = jnp.concatenate([v, jnp.zeros((8, D), F32)], axis=0)
            n2[pl.ds(24 * k, v.shape[0])] = v.astype(BF)
        rows = pl.ds(0, 24 * count + 8 * (count % 2))
        total = None
        for c in range(FFH // HID):
            u = dot(n2[rows], wup[:, c * HID:(c + 1) * HID])
            more = dot(gelu(u).astype(BF), wdown[c * HID:(c + 1) * HID])
            total = more if total is None else total + more
        for k, (r, h, _) in enumerate(pieces):
            x[r, pl.ds(3 * h, 3)] = (part(r, h) + total[24 * k:24 * k + 24]).reshape(3, 8, D)

    def span(k, h, o):
        return [(3 + 6 * k + i, h, o + 24 * i) for i in range(6)]

    def pair_step(k):
        fwd_pair(k).wait_recv()
        t = [dot(pa[...], jnp.concatenate(
            [own_a[k, pl.ds(48 * m, 48)], recv_a[k, pl.ds(48 * m, 48)]], axis=0)) for m in range(3)]
        project_in(jnp.concatenate(
            [t[m][24 * s:24 * s + 24] for s in range(4) for m in range(3)], axis=0).astype(BF))
        attend(False)
        for m in range(3):
            t = dot(pat[...], jnp.concatenate(
                [ctx[pl.ds(72 * s + 24 * m, 24)] for s in range(4)], axis=0).astype(BF))
            keep_a[k, pl.ds(48 * m, 48)] = t[:48].astype(BF)
            back_a[k, pl.ds(48 * m, 48)] = t[48:].astype(BF)
        ret_pair(k).start()

    for n in range(3):
        wcp[n].wait()
    pair_step(far)
    for n in (3, 4):
        for c in loads[n]:
            c.wait()
    own_c[...] = norm_parts((15, 16, 17), 0)
    fill(own_a, near, far)
    for c in fwd:
        c.wait_recv()
    wcp[3].wait()
    wcp[4].wait()
    project_in(dot(ps[...], jnp.concatenate(
        [own_c[...], recv_s[0], recv_s[1], recv_s[2]], axis=0)).astype(BF))
    attend(True)
    t = dot(pst[...], ctx[...].astype(BF))
    for m in (2, 1, 0):
        back_s[m] = t[80 * m + 80:80 * m + 160].astype(BF)
        ret[m].start()
    keep_c[...] = t[:80].astype(BF)

    pair_step(near)
    for n in range(5, 8):
        wcp[n].wait()
    ret_pair(near).wait_recv()
    finish(span(near, near, 0) + span(near, far, 144) + span(far, near, 288),
           jnp.concatenate([home_a[near], keep_a[near], keep_a[far]], axis=0))
    for c in ret:
        c.wait_recv()
    finish([(r0 + i, h, o + 24 * i) for r0, h, o in ((15, 1, 0), (0, 0, 80), (0, 1, 160)) for i in range(3)],
           jnp.concatenate([home_s[0], home_s[1], home_s[2]], axis=0))
    ret_pair(far).wait_recv()
    finish(span(far, far, 0) + [(15 + i, 0, 144 + 24 * i) for i in range(3)],
           jnp.concatenate([home_a[far], keep_c[...]], axis=0))
    for c in [fwd_pair(0), fwd_pair(1), ret_pair(0), ret_pair(1)] + fwd + ret:
        c.wait_send()


def hand_over(a, b, sems):
    copies = [pltpu.make_async_copy(
        a.at[pl.ds(3 * i, 3), :, pl.ds(4 * p, 4)], b.at[pl.ds(3 * i, 3), :, p], sems.at[i, p])
        for i in range(6) for p in range(2)]
    for c in copies:
        c.start()
    for c in copies:
        c.wait()


def solution(mesh):
    nlat, nlon = mesh.shape["lat"], mesh.shape["lon"]

    def local(latents, qkv_weight, proj_weight, up_weight, down_weight, modulation):
        consts = tables()
        vm = pltpu.VMEM
        view = latents.transpose(1, 2, 0, 3).reshape(18, 6, 2, 4, D)
        scratch = [
            vm((D, 3 * D), BF), vm((D, D), BF), vm((D, FFH), BF),
            vm((FFH, D), BF), vm((2, 2, D), F32),
            *[vm(c.shape, BF) for c in consts],
            vm((2, 144, D), BF), vm((3, 80, D), BF), vm((2, 144, D), BF),
            vm((80, D), BF), vm((2, 144, D), BF), vm((3, 80, D), BF),
            vm((144, 3 * D), BF), vm((144, D), F32), vm((2, 80, 2 * D), BF), vm((288, D), F32), vm((2, 144, D), BF),
            vm((80, D), BF),
            vm((2, 144, D), BF), vm((3, 80, D), BF), vm((2, 144, D), BF), vm((3, 80, D), BF),
            vm((432, D), BF),
            pltpu.SemaphoreType.DMA((8, 2)), pltpu.SemaphoreType.DMA((9,)),
            pltpu.SemaphoreType.DMA((10,)),
            pltpu.SemaphoreType.DMA((10,)),
        ]
        out = pl.pallas_call(
            functools.partial(kernel, nlat, nlon),
            out_shape=pltpu.VMEM((18, 6, 8, D), F32),
            in_specs=[pl.BlockSpec(memory_space=pl.ANY)] * (6 + len(consts)),
            out_specs=pl.BlockSpec(memory_space=pltpu.VMEM),
            scratch_shapes=scratch,
            compiler_params=pltpu.CompilerParams(
                collective_id=0, has_side_effects=True, vmem_limit_bytes=VM << 20),
        )(view, qkv_weight, proj_weight, up_weight, down_weight, modulation,
          *[jnp.asarray(c) for c in consts])
        out = pl.pallas_call(
            hand_over,
            out_shape=jax.ShapeDtypeStruct(view.shape, F32),
            in_specs=[pl.BlockSpec(memory_space=pltpu.VMEM)],
            out_specs=pl.BlockSpec(memory_space=pl.ANY),
            scratch_shapes=[pltpu.SemaphoreType.DMA((6, 2))],
            compiler_params=pltpu.CompilerParams(vmem_limit_bytes=16 << 20),
        )(out)
        return out.reshape(18, 12, 4, D).transpose(2, 0, 1, 3)

    placed = (P(None, "lat", "lon", None), P(), P(), P(), P(), P())
    return jax.shard_map(
        local, mesh=mesh, in_specs=placed, out_specs=P(None, "lat", "lon", None), check_vma=False)
```

```python
import functools
import math

import jax
import jax.numpy as jnp
import numpy as np
from jax import lax
from jax.experimental import pallas as pl
from jax.experimental.pallas import tpu as pltpu
from jax.sharding import PartitionSpec as P

HEADS = 16
D = 512
FFH = 2048
UNROLL = 4
VM = 60
HID = 1024
NEG = -1e30
BF = jnp.bfloat16
F32 = jnp.float32
MESH = pl.DeviceIdType.MESH
SLOT = {1: 0, 2: 1, 3: 2, 0: 3}
CLASSES = ((3, 6), (9, 6), (15, 3), (0, 3))


@functools.cache
def tables():
    pa = np.zeros((96, 96), np.float32)
    count = [0] * 4
    for h in range(2):
        for i in range(12):
            for lev in range(4):
                slot = SLOT[lev]
                pa[slot * 24 + count[slot], h * 48 + i * 4 + lev] = 1
                count[slot] += 1
    ps = np.zeros((288, 320), np.float32)
    count = [0] * 4
    for piece in range(4):
        for i in range(18):
            for lev in range(4):
                slot = SLOT[lev]
                ps[slot * 72 + count[slot], piece * 80 + i * 4 + lev] = 1
                count[slot] += 1
    bf = jnp.bfloat16
    return pa.astype(bf), pa.T.astype(bf), ps.astype(bf), ps.T.astype(bf)


def dot(a, b):
    return jnp.dot(a, b, preferred_element_type=F32)


def norm_mod(v, mod):
    mean = jnp.sum(v, axis=-1, keepdims=True) * (1.0 / D)
    c = v - mean
    var = jnp.sum(c * c, axis=-1, keepdims=True) * (1.0 / D)
    return (c * lax.rsqrt(var + 1e-5)) * (1.0 + mod[0:1]) + mod[1:2]


def gelu(u):
    return 0.5 * u * (1.0 + lax.erf(u * (1.0 / math.sqrt(2.0))))


def kernel(
    nlat, nlon,
    lat_hbm, wqkv_hbm, wproj_hbm, wup_hbm, wdown_hbm, mod_hbm,
    pa_hbm, pat_hbm, ps_hbm, pst_hbm,
    x,
    wqkv, wproj, wup, wdown, mod, pa, pat, ps, pst,
    send_a, send_s, own_a, own_c, recv_a, recv_s,
    qkv0, q1, kv1, ctx, keep_a, keep_c, back_a, back_s, home_a, home_s, n2,
    in_sem, w_sem, ss, rs,
):
    d, j = lax.axis_index("lat"), lax.axis_index("lon")
    up_d, dn_d = lax.rem(d + 1, nlat), lax.rem(d + nlat - 1, nlat)
    rt, lf = lax.rem(j + 1, nlon), lax.rem(j + nlon - 1, nlon)
    barrier = pltpu.get_barrier_semaphore()
    for who in ((d, rt), (d, lf), (up_d, j), (dn_d, j), (up_d, lf), (dn_d, rt)):
        pl.semaphore_signal(barrier, inc=1, device_id=who, device_id_type=MESH)

    mod_cp = pltpu.make_async_copy(mod_hbm, mod, w_sem.at[0])
    mod_cp.start()
    near, far = 1 - lax.rem(j, 2), lax.rem(j, 2)

    def load(n, r0, count, h):
        return [pltpu.make_async_copy(
            lat_hbm.at[pl.ds(r0, count), pl.ds(3 * h, 3), p],
            x.at[pl.ds(r0, count), pl.ds(3 * h, 3), pl.ds(4 * p, 4)], in_sem.at[n, p]) for p in range(2)]

    loads = [load(0, 3 + 6 * far, 6, far), load(1, 3 + 6 * near, 6, near), load(2, 3 + 6 * far, 6, near),
             load(3, 3 + 6 * near, 6, far), load(4, 15, 3, 0), load(5, 15, 3, 1), load(6, 0, 3, 0), load(7, 0, 3, 1)]
    for cs in loads:
        for c in cs:
            c.start()
    wcp = []
    for i, (a, b) in enumerate((
        (pa_hbm, pa), (wqkv_hbm, wqkv), (pat_hbm, pat), (ps_hbm, ps), (pst_hbm, pst),
        (wproj_hbm, wproj), (wup_hbm, wup), (wdown_hbm, wdown),
    )):
        wcp.append(pltpu.make_async_copy(a, b, w_sem.at[i + 1]))
        wcp[-1].start()

    def remote(src, dst, n, who):
        return pltpu.make_async_remote_copy(
            src_ref=src, dst_ref=dst, send_sem=ss.at[n], recv_sem=rs.at[n],
            device_id=who, device_id_type=MESH)

    right, left, down, above = (d, rt), (d, lf), (dn_d, j), (up_d, j)

    def fwd_pair(k):
        return remote(send_a.at[k], recv_a.at[k], k, (d, jnp.where(k == 0, lf, rt)))

    def ret_pair(k):
        return remote(back_a.at[k], home_a.at[k], 5 + k, (d, jnp.where(k == 0, rt, lf)))

    fwd = [
        remote(send_s.at[0], recv_s.at[0], 2, right),
        remote(send_s.at[1], recv_s.at[1], 3, down),
        remote(send_s.at[2], recv_s.at[2], 4, (dn_d, rt)),
    ]
    ret = [
        remote(back_s.at[0], home_s.at[0], 7, left),
        remote(back_s.at[1], home_s.at[1], 8, above),
        remote(back_s.at[2], home_s.at[2], 9, (up_d, lf)),
    ]

    mod_cp.wait()

    def part(r, h):
        return x[r, pl.ds(3 * h, 3)].reshape(24, D)

    def norm_parts(rows, h):
        v = norm_mod(jnp.concatenate([part(r, h) for r in rows], axis=0), mod[0])
        if len(rows) == 3:
            v = jnp.concatenate([v, jnp.zeros((8, D), F32)], axis=0)
        return v.astype(BF)

    def fill(dst, k, h):
        for m in range(3):
            r = 3 + 6 * k + 2 * m
            dst[k, pl.ds(48 * m, 48)] = norm_parts((r, r + 1), h)

    for n, r0, h, dst in ((7, 0, 1, 2), (6, 0, 0, 1), (5, 15, 1, 0)):
        for c in loads[n]:
            c.wait()
        send_s[dst] = norm_parts((r0, r0 + 1, r0 + 2), h)
    pl.semaphore_wait(barrier, 6)
    for c in (fwd[2], fwd[1], fwd[0]):
        c.start()
    for c in loads[0]:
        c.wait()
    fill(send_a, far, far)
    fwd_pair(far).start()
    for c in loads[1]:
        c.wait()
    fill(send_a, near, near)
    fwd_pair(near).start()
    for c in loads[2]:
        c.wait()
    fill(own_a, far, near)

    scale = math.log2(math.e) / math.sqrt(D // HEADS)
    lane = lax.broadcasted_iota(jnp.int32, (1, 128), 1)
    inside = [(lane >= 32 * h) & (lane < 32 * h + 32) for h in range(4)]
    cut = jnp.where(d == nlat - 1, NEG, 0.0)

    def apart(n):
        a = lax.rem(lax.broadcasted_iota(jnp.int32, (n, n), 0), 72) < 36
        b = lax.rem(lax.broadcasted_iota(jnp.int32, (n, n), 1), 72) < 36
        return jnp.where(a != b, cut, 0.0)

    def heads(q, kk, v, bias):
        n = kk.shape[0]
        q4 = jnp.concatenate([q * inside[h].astype(F32).astype(q.dtype) for h in range(4)], axis=0)
        s4 = lax.dot_general(q4.astype(BF), kk, (((1,), (1,)), ((), ())), preferred_element_type=F32)
        p4 = []
        for h in range(4):
            s = s4[n * h:n * h + n]
            if bias is not None:
                s = s + bias
            p4.append(jnp.exp2(s - jnp.max(s, axis=-1, keepdims=True)))
        o4 = dot(jnp.concatenate(p4, axis=0).astype(BF),
                 jnp.concatenate([v, jnp.ones((n, 128), BF)], axis=1))
        top, low = o4[:n, :128], o4[:n, 128:]
        for h in range(1, 4):
            top = jnp.where(inside[h], o4[n * h:n * h + n, :128], top)
            low = jnp.where(inside[h], o4[n * h:n * h + n, 128:], low)
        return top * (1.0 / low)

    def attend(masked):
        def step(i, carry):
            cols = [pl.ds(pl.multiple_of(512 * m + i * 128, 128), 128) for m in range(3)]
            ctx[pl.ds(0, 144), cols[0]] = heads(
                *[qkv0[:, c] for c in cols], apart(144) if masked else None)
            for m in range(2):
                ctx[pl.ds(144 + 72 * m, 72), cols[0]] = heads(
                    q1[pl.ds(72 * m, 72), cols[0]], *[kv1[m, pl.ds(0, 72), c] for c in cols[:2]],
                    apart(72) if masked else None)
            return carry

        lax.fori_loop(0, 4, step, 0, unroll=UNROLL)

    def project_in(rows):
        for c in range(3):
            cols = slice(c * D, (c + 1) * D)
            y = dot(rows, wqkv[:, cols])
            if c == 0:
                y = y * scale
            qkv0[:, cols] = y[:144].astype(BF)
            if c == 0:
                q1[...] = y[144:]
            else:
                for m in range(2):
                    kv1[m, pl.ds(0, 72), slice((c - 1) * D, c * D)] = y[144 + 72 * m:216 + 72 * m].astype(BF)


    def finish(pieces, context):
        attn = dot(context, wproj[...])
        count = len(pieces)
        for k in range(0, count, 2):
            pair = pieces[k:k + 2]
            mid = jnp.concatenate([part(r, h) + attn[o:o + 24] for r, h, o in pair], axis=0)
            for m, (r, h, _) in enumerate(pair):
                x[r, pl.ds(3 * h, 3)] = mid[24 * m:24 * m + 24].reshape(3, 8, D)
            v = norm_mod(mid, mod[1])
            if len(pair) == 1:
                v = jnp.concatenate([v, jnp.zeros((8, D), F32)], axis=0)
            n2[pl.ds(24 * k, v.shape[0])] = v.astype(BF)
        rows = pl.ds(0, 24 * count + 8 * (count % 2))
        total = None
        for c in range(FFH // HID):
            u = dot(n2[rows], wup[:, c * HID:(c + 1) * HID])
            more = dot(gelu(u).astype(BF), wdown[c * HID:(c + 1) * HID])
            total = more if total is None else total + more
        for k, (r, h, _) in enumerate(pieces):
            x[r, pl.ds(3 * h, 3)] = (part(r, h) + total[24 * k:24 * k + 24]).reshape(3, 8, D)

    def span(k, h, o):
        return [(3 + 6 * k + i, h, o + 24 * i) for i in range(6)]

    def pair_step(k):
        fwd_pair(k).wait_recv()
        t = [dot(pa[...], jnp.concatenate(
            [own_a[k, pl.ds(48 * m, 48)], recv_a[k, pl.ds(48 * m, 48)]], axis=0)) for m in range(3)]
        project_in(jnp.concatenate(
            [t[m][24 * s:24 * s + 24] for s in range(4) for m in range(3)], axis=0).astype(BF))
        attend(False)
        for m in range(3):
            t = dot(pat[...], jnp.concatenate(
                [ctx[pl.ds(72 * s + 24 * m, 24)] for s in range(4)], axis=0).astype(BF))
            keep_a[k, pl.ds(48 * m, 48)] = t[:48].astype(BF)
            back_a[k, pl.ds(48 * m, 48)] = t[48:].astype(BF)
        ret_pair(k).start()

    for n in range(3):
        wcp[n].wait()
    pair_step(far)
    for n in (3, 4):
        for c in loads[n]:
            c.wait()
    own_c[...] = norm_parts((15, 16, 17), 0)
    fill(own_a, near, far)
    for c in fwd:
        c.wait_recv()
    wcp[3].wait()
    wcp[4].wait()
    project_in(dot(ps[...], jnp.concatenate(
        [own_c[...], recv_s[0], recv_s[1], recv_s[2]], axis=0)).astype(BF))
    attend(True)
    t = dot(pst[...], ctx[...].astype(BF))
    for m in (2, 1, 0):
        back_s[m] = t[80 * m + 80:80 * m + 160].astype(BF)
        ret[m].start()
    keep_c[...] = t[:80].astype(BF)

    pair_step(near)
    for n in range(5, 8):
        wcp[n].wait()
    ret_pair(near).wait_recv()
    finish(span(near, near, 0) + span(near, far, 144) + span(far, near, 288),
           jnp.concatenate([home_a[near], keep_a[near], keep_a[far]], axis=0))
    for c in ret:
        c.wait_recv()
    finish([(r0 + i, h, o + 24 * i) for r0, h, o in ((15, 1, 0), (0, 0, 80), (0, 1, 160)) for i in range(3)],
           jnp.concatenate([home_s[0], home_s[1], home_s[2]], axis=0))
    ret_pair(far).wait_recv()
    finish(span(far, far, 0) + [(15 + i, 0, 144 + 24 * i) for i in range(3)],
           jnp.concatenate([home_a[far], keep_c[...]], axis=0))
    for c in [fwd_pair(0), fwd_pair(1), ret_pair(0), ret_pair(1)] + fwd + ret:
        c.wait_send()


def hand_over(a, b, sems):
    copies = [pltpu.make_async_copy(
        a.at[pl.ds(3 * i, 3), :, pl.ds(4 * p, 4)], b.at[pl.ds(3 * i, 3), :, p], sems.at[i, p])
        for i in range(6) for p in range(2)]
    for c in copies:
        c.start()
    for c in copies:
        c.wait()


def solution(mesh):
    nlat, nlon = mesh.shape["lat"], mesh.shape["lon"]

    def local(latents, qkv_weight, proj_weight, up_weight, down_weight, modulation):
        consts = tables()
        vm = pltpu.VMEM
        view = latents.transpose(1, 2, 0, 3).reshape(18, 6, 2, 4, D)
        scratch = [
            vm((D, 3 * D), BF), vm((D, D), BF), vm((D, FFH), BF),
            vm((FFH, D), BF), vm((2, 2, D), F32),
            *[vm(c.shape, BF) for c in consts],
            vm((2, 144, D), BF), vm((3, 80, D), BF), vm((2, 144, D), BF),
            vm((80, D), BF), vm((2, 144, D), BF), vm((3, 80, D), BF),
            vm((144, 3 * D), BF), vm((144, D), F32), vm((2, 80, 2 * D), BF), vm((288, D), F32), vm((2, 144, D), BF),
            vm((80, D), BF),
            vm((2, 144, D), BF), vm((3, 80, D), BF), vm((2, 144, D), BF), vm((3, 80, D), BF),
            vm((432, D), BF),
            pltpu.SemaphoreType.DMA((8, 2)), pltpu.SemaphoreType.DMA((9,)),
            pltpu.SemaphoreType.DMA((10,)),
            pltpu.SemaphoreType.DMA((10,)),
        ]
        out = pl.pallas_call(
            functools.partial(kernel, nlat, nlon),
            out_shape=pltpu.VMEM((18, 6, 8, D), F32),
            in_specs=[pl.BlockSpec(memory_space=pl.ANY)] * (6 + len(consts)),
            out_specs=pl.BlockSpec(memory_space=pltpu.VMEM),
            scratch_shapes=scratch,
            compiler_params=pltpu.CompilerParams(
                collective_id=0, has_side_effects=True, vmem_limit_bytes=VM << 20),
        )(view, qkv_weight, proj_weight, up_weight, down_weight, modulation,
          *[jnp.asarray(c) for c in consts])
        out = pl.pallas_call(
            hand_over,
            out_shape=jax.ShapeDtypeStruct(view.shape, F32),
            in_specs=[pl.BlockSpec(memory_space=pltpu.VMEM)],
            out_specs=pl.BlockSpec(memory_space=pl.ANY),
            scratch_shapes=[pltpu.SemaphoreType.DMA((6, 2))],
            compiler_params=pltpu.CompilerParams(vmem_limit_bytes=16 << 20),
        )(out)
        return out.reshape(18, 12, 4, D).transpose(2, 0, 1, 3)

    placed = (P(None, "lat", "lon", None), P(), P(), P(), P(), P())
    return jax.shard_map(
        local, mesh=mesh, in_specs=placed, out_specs=P(None, "lat", "lon", None), check_vma=False)
```
